256 devices in a mesh: row: 32 (over z, x_hi, core), col: 8 (over x_lo, y).
Axes of the slice: x: 4 (x_hi: 2, x_lo: 2; x = x_hi * 2 + x_lo), y: 4, z: 8, core: 2. Of those that a mesh axis runs over, the one named last changes fastest.
Arguments:
- features: bfloat16 [131072, 128], P(('row', 'col')), may hold values from -6 to 6
- weight: bfloat16 [128, 128], replicated, may hold values from -0.5 to 0.5
- adj_values: bfloat16 [32, 8, 256, 128, 128], P('row', 'col'), may hold values from -0.15625 to 0.15625
- block_coords: int32 [32, 8, 2, 256], P('row', 'col'), may hold values from 0 to 127, as said below
- block_counts: int32 [32, 8], P('row', 'col'), may hold values from 32 to 256, as said below
- cotangent: bfloat16 [131072, 128], P(('row', 'col')), may hold values from -6 to 6
Outputs:
- activated: bfloat16 [131072, 128], P(('row', 'col'))
- feature_grad: bfloat16 [131072, 128], P(('row', 'col'))
- weight_grad: float32 [128, 128], replicated
The draws below stay inside these ranges and needn't reach their ends.
Inputs may be any that keep to these rules, and one draw needn't show every extreme that they name: `block_coords`: entry [g, h, 0, s] is a block-row of row group g (below 32); entry [g, h, 1, s] a block-column of column group h (below 128); blocks may repeat. `block_counts`: some device uses all 256 slots.
All inputs are finite; a program needn't handle non-finite values.
Results may differ from the reference program's by a relative error of at most 0.0065.
Values may be sent and summed in bfloat16 or wider, within the bound.
No kernel may reach another device: no remote copies, remote signals or barrier semaphores. Data moves between devices by JAX's collectives and lax.ppermute only.
A program may use at most 128 MiB of HBM per device.

```python
import jax
import jax.numpy as jnp
from jax import lax

HID = 128
BLOCK = 128
NODE_DEV = 512
BPD = 4
ROW_BLOCKS = 32
COL_BLOCKS = 128
SLOTS = 256
NODES = 131072
N_ROW = 32
N_COL = 8
DEVICES = 256


def draw_block_coords(key, part):
    key = jax.random.fold_in(key, 11)
    key_rows, key_spread, key_offset, key_within = jax.random.split(key, 4)
    grid_shape = (N_ROW, N_COL, SLOTS)
    row_ids = jax.random.randint(key_rows, grid_shape, 0, ROW_BLOCKS)
    spread = jax.random.randint(key_spread, grid_shape, 0, COL_BLOCKS)
    offset = jax.random.randint(key_offset, grid_shape, -1, 2)
    within = jax.random.randint(key_within, grid_shape, 0, BPD)
    own_group = jnp.arange(N_ROW, dtype=jnp.int32)[:, None, None]
    band_ids = (own_group + offset) % N_ROW * BPD + within
    banded = (jnp.arange(SLOTS, dtype=jnp.int32) % 2 == 0)[None, None, :]
    col_ids = jnp.where(banded, band_ids, spread)
    return jnp.stack([row_ids, col_ids], axis=2).astype(jnp.int32)


def draw_block_counts(key, part):
    key = jax.random.fold_in(key, 23)
    key_halving, key_busiest = jax.random.split(key, 2)
    halving = jax.random.randint(key_halving, (N_ROW, N_COL), 0, 4)
    counts = jnp.right_shift(jnp.full((N_ROW, N_COL), SLOTS, jnp.int32), halving)
    busiest = jax.random.randint(key_busiest, (), 0, N_ROW * N_COL)
    flat_ids = jnp.arange(N_ROW * N_COL, dtype=jnp.int32).reshape(N_ROW, N_COL)
    return jnp.where(flat_ids == busiest, SLOTS, counts).astype(jnp.int32)


def steps_of(own_key, extent, cuts, low, largest):
    level = 1.0
    for position, shards_of in cuts:
        draws = jax.random.uniform(jax.random.fold_in(jax.random.fold_in(own_key, 6), position), (shards_of,), jnp.float32, low / len(cuts), largest / len(cuts))
        level = level * jnp.repeat(jnp.exp(draws), extent[position] // shards_of).reshape((-1,) + (1,) * (len(extent) - 1 - position))
    return level


def normal_values(stream_key, dims, width, most, pieces=(), kind=jnp.bfloat16):
    values = jax.random.normal(stream_key, dims, jnp.float32) * width
    if len(pieces) > 0:
        values = steps_of(stream_key, dims, pieces, -0.22, 0.18) * values
    return jnp.clip(values, min=-most, max=most).astype(kind)


def setup_inputs(seed: int = 0) -> dict:
    seeds = jax.random.split(jax.random.key(seed), 7)
    features = normal_values(seeds[0], (NODES, HID), 1.0, 6.0, ((0, 256),))
    weight = normal_values(seeds[1], (HID, HID), HID ** -0.5, 0.5)
    adj_values = normal_values(seeds[2], (N_ROW, N_COL, SLOTS, BLOCK, BLOCK), ((BLOCK * DEVICES // 4) ** -0.5), 0.15625, ((0, 32), (1, 8)))
    block_coords = draw_block_coords(jax.random.fold_in(seeds[6], 71), 0)
    block_counts = draw_block_counts(jax.random.fold_in(seeds[6], 71), 0)
    cotangent = normal_values(seeds[5], (NODES, HID), 1.0, 6.0, ((0, 256),))
    return dict(features=features, weight=weight, adj_values=adj_values, block_coords=block_coords, block_counts=block_counts, cotangent=cotangent)


def silu_grad(values):
    sigmoid_z = jax.nn.sigmoid(values)
    return sigmoid_z * (1.0 + values * (1.0 - sigmoid_z))

def reference(features, weight, adj_values, block_coords, block_counts, cotangent):
    hidden = jnp.dot(features, weight, preferred_element_type=jnp.float32).astype(jnp.bfloat16)
    col_ordered = jnp.transpose(hidden.reshape(N_ROW, N_COL, NODE_DEV, HID), (1, 0, 2, 3)).reshape(N_COL, COL_BLOCKS, BLOCK, HID)
    blocks_all = adj_values.reshape(N_ROW * N_COL, SLOTS, BLOCK, BLOCK)
    coords_all = block_coords.reshape(N_ROW * N_COL, 2, SLOTS)
    counts_all = block_counts.reshape(N_ROW * N_COL)
    slot_ids = jnp.arange(SLOTS, dtype=jnp.int32)
    device_ids = jnp.arange(N_ROW * N_COL, dtype=jnp.int32)

    def forward_step(running, scan_item):
        device_index, blocks, coords, block_total = scan_item
        row_group = device_index // N_COL
        col_group = device_index % N_COL
        source = col_ordered[col_group][coords[1]]
        products = jnp.einsum('sab,sbh->sah', blocks.astype(jnp.float32), source.astype(jnp.float32))
        products = jnp.where((slot_ids < block_total)[:, None, None], products, jnp.float32(0.0))
        placed = jax.ops.segment_sum(products, coords[0], num_segments=ROW_BLOCKS)
        return (running.at[row_group].add(placed), None)
    start_fwd = jnp.zeros((N_ROW, ROW_BLOCKS, BLOCK, HID), jnp.float32)
    preact, _ = lax.scan(forward_step, start_fwd, (device_ids, blocks_all, coords_all, counts_all))
    preact = preact.reshape(NODES, HID)
    activated = jax.nn.silu(preact).astype(jnp.bfloat16)
    delta = (cotangent.astype(jnp.float32) * silu_grad(preact)).astype(jnp.bfloat16)
    row_ordered = delta.reshape(N_ROW, ROW_BLOCKS, BLOCK, HID)

    def backward_step(running, scan_item):
        device_index, blocks, coords, block_total = scan_item
        row_group = device_index // N_COL
        col_group = device_index % N_COL
        source = row_ordered[row_group][coords[0]]
        products = jnp.einsum('sab,sah->sbh', blocks.astype(jnp.float32), source.astype(jnp.float32))
        products = jnp.where((slot_ids < block_total)[:, None, None], products, jnp.float32(0.0))
        placed = jax.ops.segment_sum(products, coords[1], num_segments=COL_BLOCKS)
        return (running.at[col_group].add(placed), None)
    start_bwd = jnp.zeros((N_COL, COL_BLOCKS, BLOCK, HID), jnp.float32)
    grad_cols, _ = lax.scan(backward_step, start_bwd, (device_ids, blocks_all, coords_all, counts_all))
    grad_hidden = jnp.transpose(grad_cols.reshape(N_COL, N_ROW, NODE_DEV, HID), (1, 0, 2, 3)).reshape(NODES, HID)
    grad_rounded = grad_hidden.astype(jnp.bfloat16)
    feature_grad = jnp.dot(grad_rounded, weight.T, preferred_element_type=jnp.float32).astype(jnp.bfloat16)
    weight_grad = jnp.dot(features.T, grad_rounded, preferred_element_type=jnp.float32) * NODES ** (-0.5)
    return (activated, feature_grad, weight_grad)
```

```python
import jax
import jax.numpy as jnp
from jax import lax
from jax.experimental import pallas as pl
from jax.experimental.pallas import tpu as pltpu
from jax.sharding import PartitionSpec as P

NZ = 8
BLK = 128
BPD = 4
HALF = 2
CHUNK = 32
UNROLL = 16
VMEM_LIMIT = 24 << 20
BF = jnp.bfloat16
F32 = jnp.float32

PLACES = ((0, 4), (8, 16), (20, 32), (36, 48), (52, 60), (40, 56), (24, 44), (12, 28))


def silu_grad(values):
    sigmoid_z = jax.nn.sigmoid(values)
    return sigmoid_z * (1.0 + values * (1.0 - sigmoid_z))


def wide(value):
    return value.astype(F32)


def cat(*values):
    return jnp.concatenate(values, axis=0)


def z_shift(value, step):
    perm = [(r, ((r // 4 + step) % NZ) * 4 + r % 4) for r in range(4 * NZ)]
    return lax.ppermute(value, "row", perm)


def row_swap(value, mask):
    return lax.ppermute(value, "row", [(r, r ^ mask) for r in range(4 * NZ)])


def split(value):
    high = value.astype(BF)
    return high, (value - wide(high)).astype(BF)


def add_products(x_first, dst, src, count, blocks, held, acc, slots, sems):
    per_chunk = CHUNK // UNROLL
    groups = (jnp.clip(count[0], 0, slots.shape[0]) + UNROLL - 1) // UNROLL

    def body(j, carry):
        products = []
        for u in range(UNROLL):
            s = j * UNROLL + u
            a, x = slots[s], held[src[s]]
            pair = (x, a) if x_first else (a, x)
            products.append(jnp.dot(*pair, preferred_element_type=F32))
        for u in range(UNROLL):
            acc[dst[j * UNROLL + u]] += products[u]
        return carry

    def chunk(c, carry):
        load(blocks, slots, sems, c).wait()
        lax.fori_loop(c * per_chunk, jnp.minimum((c + 1) * per_chunk, groups), body, 0)
        return carry

    lax.fori_loop(0, slots.shape[0] // CHUNK, chunk, 0)


def load(blocks, slots, sems, c):
    part = pl.ds(c * CHUNK, CHUNK)
    return pltpu.make_async_copy(blocks.at[part], slots.at[part], sems.at[c])


def forward_kernel(dst, src, count, blocks, *refs):
    pieces, (out, acc, held, slots, sems, piece_sems) = refs[:-6], refs[-6:]
    for c in range(slots.shape[0] // CHUNK):
        load(blocks, slots, sems, c).start()
    copies, at = [], 0
    for k, piece in enumerate(pieces):
        size = piece.shape[0]
        copies.append(
            pltpu.make_async_copy(piece, held.at[pl.ds(at, size)], piece_sems.at[k])
        )
        at += size
    for copy in copies:
        copy.start()
    acc[...] = jnp.zeros_like(acc)
    for copy in copies:
        copy.wait()
    add_products(False, dst, src, count, blocks, held, acc, slots, sems)
    out[...] = acc[: out.shape[0]].astype(out.dtype)


def backward_kernel(dst, src, count, blocks, every, keep, send, sums, acc, slots, sems):
    for c in range(slots.shape[0] // CHUNK):
        load(blocks, slots, sems, c).start()
    acc[...] = jnp.zeros_like(acc)
    span = BPD + 1
    total = wide(every[BPD])
    for k in range(1, every.shape[0] // span):
        total = total + wide(every[k * span + BPD])
    high, low = split(total)
    half = keep.shape[0]
    send[half], send[half + 1] = high, low
    sums[...] = wide(high) + wide(low)
    add_products(True, dst, src, count, blocks, every, acc, slots, sems)
    keep[...] = acc[:half].astype(keep.dtype)
    send[:half] = acc[half : 2 * half].astype(send.dtype)


def product(kernel, name, blocks, dst, src, count, sources, out_shape, source_space, scratch):
    vmem = pl.BlockSpec(memory_space=pltpu.VMEM)
    smem = pl.BlockSpec(memory_space=pltpu.SMEM)
    slots = blocks.shape[0]
    return pl.pallas_call(
        kernel,
        name=name,
        in_specs=[smem] * 3
        + [pl.BlockSpec(memory_space=pltpu.HBM)]
        + [pl.BlockSpec(memory_space=source_space)] * len(sources),
        out_specs=[vmem] * len(out_shape),
        out_shape=out_shape,
        scratch_shapes=scratch,
        compiler_params=pltpu.CompilerParams(vmem_limit_bytes=VMEM_LIMIT),
        cost_estimate=pl.CostEstimate(
            flops=2 * slots * BLK**3, bytes_accessed=14 << 20, transcendentals=0
        ),
    )(dst, src, count, pltpu.with_memory_space_constraint(blocks, pltpu.HBM), *sources)


def forward_product(blocks, dst, src, count, pieces, num_dst):
    slots = blocks.shape[0]
    held = sum(piece.shape[0] for piece in pieces)
    (out,) = product(
        forward_kernel,
        "forward_product",
        blocks,
        dst,
        src,
        count,
        pieces,
        [jax.ShapeDtypeStruct((num_dst, BLK, BLK), BF)],
        pl.ANY,
        [
            pltpu.VMEM((num_dst + 1, BLK, BLK), F32),
            pltpu.VMEM((held, BLK, BLK), BF),
            pltpu.VMEM(blocks.shape, BF),
            pltpu.SemaphoreType.DMA((slots // CHUNK,)),
            pltpu.SemaphoreType.DMA((len(pieces),)),
        ],
    )
    return out


def backward_product(blocks, dst, src, count, every, num_dst):
    slots = blocks.shape[0]
    half = num_dst // 2
    return product(
        backward_kernel,
        "backward_product",
        blocks,
        dst,
        src,
        count,
        [every],
        [
            jax.ShapeDtypeStruct((half, BLK, BLK), BF),
            jax.ShapeDtypeStruct((half + 2, BLK, BLK), BF),
            jax.ShapeDtypeStruct((BLK, BLK), F32),
        ],
        pltpu.VMEM,
        [
            pltpu.VMEM((num_dst + 1, BLK, BLK), F32),
            pltpu.VMEM(blocks.shape, BF),
            pltpu.SemaphoreType.DMA((slots // CHUNK,)),
        ],
    )


def gather_rows(own):
    mate = row_swap(own, 2)
    up1, down1 = z_shift(own, 1), z_shift(own, -1)
    up2, down2 = z_shift(cat(mate, up1), 1), z_shift(cat(down1, mate), -1)
    up3, down3 = z_shift(up2, 1), z_shift(down2, -1)
    up4, down4 = z_shift(up3[: BPD + HALF], 1), z_shift(down3[HALF:], -1)
    up5, down5 = z_shift(up4[:HALF], 1), z_shift(down4[BPD:], -1)
    groups = [
        cat(own, mate, up1, down1),
        cat(up2, down2),
        cat(up3, down3),
        cat(up4, down4),
        cat(up5, down5),
    ]
    return groups + [row_swap(group, 1) for group in groups]


def scatter_rows(keep, send, sums):
    arrived = row_swap(send, 1)
    half = keep.shape[0]
    tag = (sums + wide(arrived[half]) + wide(arrived[half + 1])).astype(BF)[None]
    seen_up, seen_down = [], []

    def term(d, x, lo=0, hi=BPD):
        at = (2 * d + x) * BPD
        return wide(keep[at + lo : at + hi]) + wide(arrived[at + lo : at + hi])

    def step(up, down, up_tag, down_tag):
        up = cat(*[part.astype(BF) for part in up], up_tag)
        down = cat(*[part.astype(BF) for part in down], down_tag)
        up, down = lax.optimization_barrier((up, down))
        up, down = z_shift(up, 1), z_shift(down, -1)
        seen_up.append(up[-1:])
        seen_down.append(down[-1:])
        return wide(up[:-1]), wide(down[:-1]), up[-1:], down[-1:]

    def front(value):
        return jnp.pad(value, ((0, HALF), (0, 0), (0, 0)))

    def back(value):
        return jnp.pad(value, ((HALF, 0), (0, 0), (0, 0)))

    up, down, ut, dt = step([term(4, 1, 0, HALF)], [term(4, 1, HALF)], tag, tag)
    up, down, ut, dt = step(
        [term(3, 1) + front(up), term(4, 0, 0, HALF)],
        [term(4, 0, HALF), term(5, 1) + back(down)],
        ut,
        dt,
    )
    up, down, ut, dt = step(
        [term(2, 1) + up[:BPD], term(3, 0) + front(up[BPD:])],
        [term(5, 0) + back(down[:HALF]), term(6, 1) + down[HALF:]],
        ut,
        dt,
    )
    up, down, ut, dt = step(
        [term(1, 1) + up[:BPD], term(2, 0) + up[BPD:]],
        [term(6, 0) + down[:BPD], term(7, 1) + down[BPD:]],
        ut,
        dt,
    )
    near = [tag] + seen_up + seen_down[: NZ // 2 - 1][::-1]
    z = lax.axis_index("row") // 4
    summed = jnp.zeros((BLK, BLK), F32)
    for k in range(NZ):
        d = (z - k) % NZ
        chosen = near[0][0]
        for n in range(1, NZ):
            chosen = jnp.where(d == n, near[n][0], chosen)
        summed = summed + wide(chosen)
    high, low = split(summed)
    theirs = term(0, 1) + up[:BPD] + down[BPD:]
    theirs = cat(theirs.astype(BF), high[None], low[None])
    up = (term(1, 0) + up[BPD:]).astype(BF)
    down = (term(7, 0) + down[:BPD]).astype(BF)
    theirs, up, down = lax.optimization_barrier((theirs, up, down))
    mate, up, down = row_swap(theirs, 2), z_shift(up, 1), z_shift(down, -1)
    total = term(0, 0) + wide(mate[:BPD]) + wide(up) + wide(down)
    return total, (wide(high) + wide(low)) + (wide(mate[BPD]) + wide(mate[BPD + 1]))


def per_device(features, weight, adj_values, block_coords, block_counts, cotangent):
    blocks = adj_values[0, 0]
    coords = block_coords[0, 0]
    count = block_counts[0]
    slots = blocks.shape[0]
    row_devices = lax.axis_size("row")
    col_devices = lax.axis_size("col")
    row_blocks = col_devices * BPD
    col_blocks = row_devices * BPD
    nodes = features.shape[0]
    dot = lambda a, b: jnp.dot(a, b, preferred_element_type=F32)

    me = lax.axis_index("row")
    owner = coords[1] // BPD
    apart = (owner ^ me) & 3
    inner = coords[1] % BPD
    core_part = (apart & 1) * (col_blocks // 2)
    distance = (me // 4 - owner // 4) % NZ * 2 + (apart >> 1)
    from_place = core_part + inner
    for k, place in enumerate(place for pair in PLACES for place in pair):
        from_place = from_place + jnp.where(distance == k, place, 0)
    to_place = core_part + (((owner // 4 - me // 4) % NZ) * 2 + (apart >> 1)) * BPD + inner
    live = jnp.arange(slots, dtype=jnp.int32) < count[0]
    forward_dst = jnp.where(live, coords[0], row_blocks)
    backward_dst = jnp.where(live, to_place, col_blocks)
    delta_at = coords[0] // BPD * (BPD + 1) + coords[0] % BPD

    pieces = gather_rows(features.reshape(BPD, BLK, BLK))
    partial = forward_product(blocks, forward_dst, from_place, count, pieces, row_blocks)
    parts = lax.all_to_all(partial.reshape(col_devices, nodes, BLK), "col", 0, 0)
    spread = jnp.sum(wide(parts), axis=0)
    high, low = split(spread)
    preact = dot(high, weight) + dot(low, weight)
    activated = jax.nn.silu(preact).astype(BF)
    delta = (wide(cotangent) * silu_grad(preact)).astype(BF)
    delta_t = jnp.swapaxes(delta.reshape(BPD, BLK, BLK), 1, 2)

    weight_part = (dot(high.T, delta) + dot(low.T, delta)).astype(BF)
    message = cat(delta_t, weight_part[None])
    every = lax.all_to_all(
        jnp.broadcast_to(message[None], (col_devices,) + message.shape), "col", 0, 0
    ).reshape(-1, BLK, BLK)
    keep, send, sums = backward_product(blocks, backward_dst, delta_at, count, every, col_blocks)
    total, weight_sum = scatter_rows(keep, send, sums)
    grad_scale = float(nodes * row_devices * col_devices) ** (-0.5)
    feature_grad = jnp.einsum("khb,ih->kbi", total.astype(BF), weight, preferred_element_type=F32)
    return activated, feature_grad.astype(BF).reshape(nodes, BLK), weight_sum * grad_scale


def solution(mesh):
    in_specs = (
        P(("row", "col"), None),
        P(),
        P("row", "col", None, None, None),
        P("row", "col", None, None),
        P("row", "col"),
        P(("row", "col"), None),
    )
    out_specs = (P(("row", "col"), None), P(("row", "col"), None), P())
    return jax.shard_map(
        per_device, mesh=mesh, in_specs=in_specs, out_specs=out_specs, check_vma=False
    )
```

```python
import jax
import jax.numpy as jnp
from jax import lax
from jax.experimental import pallas as pl
from jax.experimental.pallas import tpu as pltpu
from jax.sharding import PartitionSpec as P

NZ = 8
BLK = 128
BPD = 4
HALF = 2
CHUNK = 32
UNROLL = 32
VMEM_LIMIT = 24 << 20
BF = jnp.bfloat16
F32 = jnp.float32

PLACES = ((0, 4), (8, 16), (20, 32), (36, 48), (52, 60), (40, 56), (24, 44), (12, 28))


ORDER = (
    (4, 1), (3, 1), (5, 1), (4, 0), (2, 1), (6, 1), (3, 0), (5, 0),
    (1, 1), (7, 1), (2, 0), (6, 0), (0, 1), (1, 0), (7, 0), (0, 0),
)
SOON = 4 * BPD


def silu_grad(values):
    sigmoid_z = jax.nn.sigmoid(values)
    return sigmoid_z * (1.0 + values * (1.0 - sigmoid_z))


def wide(value):
    return value.astype(F32)


def cat(*values):
    return jnp.concatenate(values, axis=0)


def z_shift(value, step):
    perm = [(r, ((r // 4 + step) % NZ) * 4 + r % 4) for r in range(4 * NZ)]
    return lax.ppermute(value, "row", perm)


def row_swap(value, mask):
    return lax.ppermute(value, "row", [(r, r ^ mask) for r in range(4 * NZ)])


def split(value):
    high = lax.reduce_precision(value, 8, 7)
    return high.astype(BF), (value - high).astype(BF)


def add_products(x_first, dst, src, count, blocks, held, acc, slots, sems):
    per_chunk = CHUNK // UNROLL
    groups = (jnp.clip(count[0], 0, slots.shape[0]) + UNROLL - 1) // UNROLL

    def body(j, carry):
        products = []
        for u in range(UNROLL):
            s = j * UNROLL + u
            a, x = slots[s], held[src[s]]
            pair = (x, a) if x_first else (a, x)
            products.append(jnp.dot(*pair, preferred_element_type=F32))
        for u in range(UNROLL):
            acc[dst[j * UNROLL + u]] += products[u]
        return carry

    def chunk(c, carry):
        load(blocks, slots, sems, c).wait()
        lax.fori_loop(c * per_chunk, jnp.minimum((c + 1) * per_chunk, groups), body, 0)
        return carry

    lax.fori_loop(0, slots.shape[0] // CHUNK, chunk, 0)


def load(blocks, slots, sems, c):
    part = pl.ds(c * CHUNK, CHUNK)
    return pltpu.make_async_copy(blocks.at[part], slots.at[part], sems.at[c])


def forward_kernel(dst, src, count, blocks, *refs):
    pieces, (out, acc, held, slots, sems, piece_sems) = refs[:-6], refs[-6:]
    for c in range(slots.shape[0] // CHUNK):
        load(blocks, slots, sems, c).start()
    copies, at = [], 0
    for k, piece in enumerate(pieces):
        size = piece.shape[0]
        copies.append(
            pltpu.make_async_copy(piece, held.at[pl.ds(at, size)], piece_sems.at[k])
        )
        at += size
    for copy in copies:
        copy.start()
    acc[...] = jnp.zeros_like(acc)
    for copy in copies:
        copy.wait()
    add_products(False, dst, src, count, blocks, held, acc, slots, sems)
    out[...] = acc[: out.shape[0]].astype(out.dtype)


def split_here(value):
    high = value.astype(BF)
    return high, (value - wide(high)).astype(BF)


def backward_kernel(dst, src, count, blocks, every, keep, soon, later, sums, acc, slots, sems):
    for c in range(slots.shape[0] // CHUNK):
        load(blocks, slots, sems, c).start()
    acc[...] = jnp.zeros_like(acc)
    span = BPD + 1
    total = wide(every[BPD])
    for k in range(1, every.shape[0] // span):
        total = total + wide(every[k * span + BPD])
    high, low = split_here(total)
    half = keep.shape[0]
    soon[SOON], soon[SOON + 1] = high, low
    sums[...] = wide(high) + wide(low)
    add_products(True, dst, src, count, blocks, every, acc, slots, sems)
    keep[...] = acc[:half].astype(keep.dtype)
    soon[:SOON] = acc[half : half + SOON].astype(soon.dtype)
    later[...] = acc[half + SOON : 2 * half].astype(later.dtype)


def product(kernel, name, blocks, dst, src, count, sources, out_shape, source_space, scratch):
    vmem = pl.BlockSpec(memory_space=pltpu.VMEM)
    smem = pl.BlockSpec(memory_space=pltpu.SMEM)
    slots = blocks.shape[0]
    return pl.pallas_call(
        kernel,
        name=name,
        in_specs=[smem] * 3
        + [pl.BlockSpec(memory_space=pltpu.HBM)]
        + [pl.BlockSpec(memory_space=source_space)] * len(sources),
        out_specs=[vmem] * len(out_shape),
        out_shape=out_shape,
        scratch_shapes=scratch,
        compiler_params=pltpu.CompilerParams(vmem_limit_bytes=VMEM_LIMIT),
        cost_estimate=pl.CostEstimate(
            flops=2 * slots * BLK**3, bytes_accessed=14 << 20, transcendentals=0
        ),
    )(dst, src, count, pltpu.with_memory_space_constraint(blocks, pltpu.HBM), *sources)


def forward_product(blocks, dst, src, count, pieces, num_dst):
    slots = blocks.shape[0]
    held = sum(piece.shape[0] for piece in pieces)
    (out,) = product(
        forward_kernel,
        "forward_product",
        blocks,
        dst,
        src,
        count,
        pieces,
        [jax.ShapeDtypeStruct((num_dst, BLK, BLK), BF)],
        pl.ANY,
        [
            pltpu.VMEM((num_dst + 1, BLK, BLK), F32),
            pltpu.VMEM((held, BLK, BLK), BF),
            pltpu.VMEM(blocks.shape, BF),
            pltpu.SemaphoreType.DMA((slots // CHUNK,)),
            pltpu.SemaphoreType.DMA((len(pieces),)),
        ],
    )
    return out


def backward_product(blocks, dst, src, count, every, num_dst):
    slots = blocks.shape[0]
    half = num_dst // 2
    return product(
        backward_kernel,
        "backward_product",
        blocks,
        dst,
        src,
        count,
        [every],
        [
            jax.ShapeDtypeStruct((half, BLK, BLK), BF),
            jax.ShapeDtypeStruct((SOON + 2, BLK, BLK), BF),
            jax.ShapeDtypeStruct((half - SOON, BLK, BLK), BF),
            jax.ShapeDtypeStruct((BLK, BLK), F32),
        ],
        pltpu.VMEM,
        [
            pltpu.VMEM((num_dst + 1, BLK, BLK), F32),
            pltpu.VMEM(blocks.shape, BF),
            pltpu.SemaphoreType.DMA((slots // CHUNK,)),
        ],
    )


def middle_kernel(parts, weight, cotangent, activated, message):
    dot = lambda a, b: jnp.dot(a, b, preferred_element_type=F32)
    spread = wide(parts[0])
    for k in range(1, parts.shape[0]):
        spread = spread + wide(parts[k])
    high, low = split_here(spread)
    preact = dot(high, weight[...]) + dot(low, weight[...])
    activated[...] = (preact * jax.nn.sigmoid(preact)).astype(BF)
    delta = wide(cotangent[...]) * silu_grad(preact)
    rounded = delta.astype(BF)
    blocks = [delta[b * BLK : (b + 1) * BLK].T.astype(BF) for b in range(BPD)]
    blocks.append((dot(high.T, rounded) + dot(low.T, rounded)).astype(BF))
    for k in range(message.shape[0]):
        for b, block in enumerate(blocks):
            message[k, b] = block


def middle(parts, weight, cotangent):
    vmem = pl.BlockSpec(memory_space=pltpu.VMEM)
    return pl.pallas_call(
        middle_kernel,
        name="middle",
        in_specs=[vmem] * 3,
        out_specs=[vmem] * 2,
        out_shape=[
            jax.ShapeDtypeStruct(cotangent.shape, BF),
            jax.ShapeDtypeStruct((parts.shape[0], BPD + 1, BLK, BLK), BF),
        ],
        compiler_params=pltpu.CompilerParams(vmem_limit_bytes=VMEM_LIMIT),
        cost_estimate=pl.CostEstimate(
            flops=8 * cotangent.size * BLK, bytes_accessed=4 << 20, transcendentals=cotangent.size
        ),
    )(parts, weight, cotangent)


def gather_rows(own):
    mate = row_swap(own, 2)
    up1, down1 = z_shift(own, 1), z_shift(own, -1)
    up2, down2 = z_shift(cat(mate, up1), 1), z_shift(cat(down1, mate), -1)
    up3, down3 = z_shift(up2, 1), z_shift(down2, -1)
    up4, down4 = z_shift(up3[: BPD + HALF], 1), z_shift(down3[HALF:], -1)
    up5, down5 = z_shift(up4[:HALF], 1), z_shift(down4[BPD:], -1)
    groups = [cat(own, mate, up1, down1), cat(up2, down2), cat(up3, down3)]
    groups, up4, down4 = lax.optimization_barrier((groups, up4, down4))
    groups += [cat(up4, down4), cat(up5, down5)]
    return groups + [row_swap(group, 1) for group in groups]


def scatter_rows(keep, soon, later, sums):
    soon, later = row_swap(soon, 1), row_swap(later, 1)
    tag = (sums + wide(soon[SOON]) + wide(soon[SOON + 1])).astype(BF)[None]
    seen_up, seen_down = [], []

    def term(d, x, lo=0, hi=BPD):
        at = ORDER.index((d, x)) * BPD
        arrived, first = (soon, at) if at < SOON else (later, at - SOON)
        return wide(keep[at + lo : at + hi]) + wide(arrived[first + lo : first + hi])

    def step(up, down, up_tag, down_tag, ahead=()):
        up = cat(*[part.astype(BF) for part in up], up_tag)
        down = cat(*[part.astype(BF) for part in down], down_tag)
        up, down, ahead = lax.optimization_barrier((up, down, ahead))
        up, down = z_shift(up, 1), z_shift(down, -1)
        up_tag, down_tag = lax.optimization_barrier((up[-1:], down[-1:]))
        seen_up.append(up_tag)
        seen_down.append(down_tag)
        return wide(up[:-1]), wide(down[:-1]), up_tag, down_tag, ahead

    def front(value):
        return jnp.pad(value, ((0, HALF), (0, 0), (0, 0)))

    def back(value):
        return jnp.pad(value, ((HALF, 0), (0, 0), (0, 0)))

    up, down, ut, dt, _ = step([term(4, 1, 0, HALF)], [term(4, 1, HALF)], tag, tag)
    up, down, ut, dt, _ = step(
        [term(3, 1) + front(up), term(4, 0, 0, HALF)],
        [term(4, 0, HALF), term(5, 1) + back(down)],
        ut,
        dt,
    )
    up, down, ut, dt, ahead = step(
        [term(2, 1) + up[:BPD], term(3, 0) + front(up[BPD:])],
        [term(5, 0) + back(down[:HALF]), term(6, 1) + down[HALF:]],
        ut,
        dt,
        [term(1, 1), term(2, 0), term(6, 0), term(7, 1)],
    )
    up, down, ut, dt, ahead = step(
        [ahead[0] + up[:BPD], ahead[1] + up[BPD:]],
        [ahead[2] + down[:BPD], ahead[3] + down[BPD:]],
        ut,
        dt,
        [term(0, 1), term(1, 0), term(7, 0), term(0, 0)],
    )
    near = [tag] + seen_up + seen_down[: NZ // 2 - 1][::-1]
    z = lax.axis_index("row") // 4
    summed = jnp.zeros((BLK, BLK), F32)
    for k in range(NZ):
        d = (z - k) % NZ
        chosen = near[0][0]
        for n in range(1, NZ):
            chosen = jnp.where(d == n, near[n][0], chosen)
        summed = summed + wide(chosen)
    high, low = lax.optimization_barrier(split(summed))
    theirs = ahead[0] + up[:BPD] + down[BPD:]
    up = (ahead[1] + up[BPD:]).astype(BF)
    down = (ahead[2] + down[:BPD]).astype(BF)
    up, down = lax.optimization_barrier((up, down))
    theirs = cat(theirs.astype(BF), high[None], low[None])
    mate, up, down = row_swap(theirs, 2), z_shift(up, 1), z_shift(down, -1)
    total = ahead[3] + wide(mate[:BPD]) + wide(up) + wide(down)
    return total, (wide(high) + wide(low)) + (wide(mate[BPD]) + wide(mate[BPD + 1]))


def per_device(features, weight, adj_values, block_coords, block_counts, cotangent):
    blocks = adj_values[0, 0]
    coords = block_coords[0, 0]
    count = block_counts[0]
    slots = blocks.shape[0]
    row_devices = lax.axis_size("row")
    col_devices = lax.axis_size("col")
    row_blocks = col_devices * BPD
    col_blocks = row_devices * BPD
    nodes = features.shape[0]

    me = lax.axis_index("row")
    owner = coords[1] // BPD
    apart = (owner ^ me) & 3
    inner = coords[1] % BPD
    core_part = (apart & 1) * (col_blocks // 2)
    distance = (me // 4 - owner // 4) % NZ * 2 + (apart >> 1)
    from_place = core_part + inner
    for k, place in enumerate(place for pair in PLACES for place in pair):
        from_place = from_place + jnp.where(distance == k, place, 0)
    to_place = core_part + inner
    toward = (owner // 4 - me // 4) % NZ * 2 + (apart >> 1)
    for k, (d, x) in enumerate(ORDER):
        to_place = to_place + jnp.where(toward == 2 * d + x, k * BPD, 0)
    live = jnp.arange(slots, dtype=jnp.int32) < count[0]
    forward_dst = jnp.where(live, coords[0], row_blocks)
    backward_dst = jnp.where(live, to_place, col_blocks)
    delta_at = coords[0] // BPD * (BPD + 1) + coords[0] % BPD

    pieces = gather_rows(features.reshape(BPD, BLK, BLK))
    partial = forward_product(blocks, forward_dst, from_place, count, pieces, row_blocks)
    parts = lax.all_to_all(partial.reshape(col_devices, nodes, BLK), "col", 0, 0)
    activated, message = middle(parts, weight, cotangent)
    every = lax.all_to_all(message, "col", 0, 0).reshape(-1, BLK, BLK)
    total, weight_sum = scatter_rows(
        *backward_product(blocks, backward_dst, delta_at, count, every, col_blocks)
    )
    grad = lax.optimization_barrier(total.astype(BF))
    grad_scale = float(nodes * row_devices * col_devices) ** (-0.5)
    feature_grad = jnp.einsum("khb,ih->kbi", grad, weight, preferred_element_type=F32)
    return activated, feature_grad.astype(BF).reshape(nodes, BLK), weight_sum * grad_scale


def solution(mesh):
    in_specs = (
        P(("row", "col"), None),
        P(),
        P("row", "col", None, None, None),
        P("row", "col", None, None),
        P("row", "col"),
        P(("row", "col"), None),
    )
    out_specs = (P(("row", "col"), None), P(("row", "col"), None), P())
    return jax.shard_map(
        per_device, mesh=mesh, in_specs=in_specs, out_specs=out_specs, check_vma=False
    )
```

```python
import jax
import jax.numpy as jnp
from jax import lax
from jax.experimental import pallas as pl
from jax.experimental.pallas import tpu as pltpu
from jax.sharding import PartitionSpec as P

NZ = 8
BLK = 128
BPD = 4
HALF = 2
CHUNK = 32
UNROLL = 32
VMEM_LIMIT = 24 << 20
BF = jnp.bfloat16
F32 = jnp.float32

PLACES = ((0, 4), (8, 12), (24, 28), (40, 44), (56, 60), (48, 52), (32, 36), (16, 20))

ORDER = (
    (4, 1), (3, 1), (5, 1), (4, 0), (2, 1), (6, 1), (3, 0), (5, 0),
    (1, 1), (7, 1), (2, 0), (6, 0), (0, 1), (1, 0), (7, 0), (0, 0),
)
SOON = 4 * BPD


def silu_grad(values):
    sigmoid_z = jax.nn.sigmoid(values)
    return sigmoid_z * (1.0 + values * (1.0 - sigmoid_z))


def wide(value):
    return value.astype(F32)


def cat(*values):
    return jnp.concatenate(values, axis=0)


def z_shift(value, step, mask=0):
    perm = [(r, ((r // 4 + step) % NZ) * 4 + (r % 4 ^ mask)) for r in range(4 * NZ)]
    return lax.ppermute(value, "row", perm)


def row_swap(value, mask):
    return lax.ppermute(value, "row", [(r, r ^ mask) for r in range(4 * NZ)])


def split(value):
    high = value.astype(BF)
    return high, (value - wide(high)).astype(BF)


def add_products(x_first, dst, src, count, blocks, held, acc, slots, sems):
    per_chunk = CHUNK // UNROLL
    groups = (jnp.clip(count[0], 0, slots.shape[0]) + UNROLL - 1) // UNROLL

    def body(j, carry):
        products = []
        for u in range(UNROLL):
            s = j * UNROLL + u
            a, x = slots[s], held[src[s]]
            pair = (x, a) if x_first else (a, x)
            products.append(jnp.dot(*pair, preferred_element_type=F32))
        for u in range(UNROLL):
            acc[dst[j * UNROLL + u]] += products[u]
        return carry

    def chunk(c, carry):
        load(blocks, slots, sems, c).wait()
        lax.fori_loop(c * per_chunk, jnp.minimum((c + 1) * per_chunk, groups), body, 0)
        return carry

    lax.fori_loop(0, slots.shape[0] // CHUNK, chunk, 0)


def load(blocks, slots, sems, c):
    part = pl.ds(c * CHUNK, CHUNK)
    return pltpu.make_async_copy(blocks.at[part], slots.at[part], sems.at[c])


def forward_kernel(dst, src, count, blocks, *refs):
    pieces, (out, acc, held, slots, sems, piece_sems) = refs[:-6], refs[-6:]
    for c in range(slots.shape[0] // CHUNK):
        load(blocks, slots, sems, c).start()
    copies, at = [], 0
    for k, piece in enumerate(pieces):
        size = piece.shape[0]
        copies.append(
            pltpu.make_async_copy(piece, held.at[pl.ds(at, size)], piece_sems.at[k])
        )
        at += size
    for copy in copies:
        copy.start()
    acc[...] = jnp.zeros_like(acc)
    for copy in copies:
        copy.wait()
    add_products(False, dst, src, count, blocks, held, acc, slots, sems)
    out[...] = acc[: out.shape[0]].astype(out.dtype)


def backward_kernel(dst, src, count, blocks, every, keep, soon, later, sums, acc, slots, sems):
    for c in range(slots.shape[0] // CHUNK):
        load(blocks, slots, sems, c).start()
    acc[...] = jnp.zeros_like(acc)
    span = BPD + 1
    total = wide(every[BPD])
    for k in range(1, every.shape[0] // span):
        total = total + wide(every[k * span + BPD])
    high, low = split(total)
    half = keep.shape[0]
    soon[SOON], soon[SOON + 1] = high, low
    sums[...] = wide(high) + wide(low)
    add_products(True, dst, src, count, blocks, every, acc, slots, sems)
    keep[...] = acc[:half].astype(keep.dtype)
    soon[:SOON] = acc[half : half + SOON].astype(soon.dtype)
    later[...] = acc[half + SOON : 2 * half].astype(later.dtype)


def product(kernel, name, blocks, dst, src, count, sources, out_shape, source_space, scratch):
    vmem = pl.BlockSpec(memory_space=pltpu.VMEM)
    smem = pl.BlockSpec(memory_space=pltpu.SMEM)
    slots = blocks.shape[0]
    return pl.pallas_call(
        kernel,
        name=name,
        in_specs=[smem] * 3
        + [pl.BlockSpec(memory_space=pltpu.HBM)]
        + [pl.BlockSpec(memory_space=source_space)] * len(sources),
        out_specs=[vmem] * len(out_shape),
        out_shape=out_shape,
        scratch_shapes=scratch,
        compiler_params=pltpu.CompilerParams(vmem_limit_bytes=VMEM_LIMIT),
        cost_estimate=pl.CostEstimate(
            flops=2 * slots * BLK**3, bytes_accessed=14 << 20, transcendentals=0
        ),
    )(dst, src, count, pltpu.with_memory_space_constraint(blocks, pltpu.HBM), *sources)


def forward_product(blocks, dst, src, count, pieces, num_dst):
    slots = blocks.shape[0]
    held = sum(piece.shape[0] for piece in pieces)
    (out,) = product(
        forward_kernel,
        "forward_product",
        blocks,
        dst,
        src,
        count,
        [pltpu.with_memory_space_constraint(piece, pltpu.VMEM) for piece in pieces],
        [jax.ShapeDtypeStruct((num_dst, BLK, BLK), BF)],
        pltpu.VMEM,
        [
            pltpu.VMEM((num_dst + 1, BLK, BLK), F32),
            pltpu.VMEM((held, BLK, BLK), BF),
            pltpu.VMEM(blocks.shape, BF),
            pltpu.SemaphoreType.DMA((slots // CHUNK,)),
            pltpu.SemaphoreType.DMA((len(pieces),)),
        ],
    )
    return out


def backward_product(blocks, dst, src, count, every, num_dst):
    slots = blocks.shape[0]
    half = num_dst // 2
    return product(
        backward_kernel,
        "backward_product",
        blocks,
        dst,
        src,
        count,
        [every],
        [
            jax.ShapeDtypeStruct((half, BLK, BLK), BF),
            jax.ShapeDtypeStruct((SOON + 2, BLK, BLK), BF),
            jax.ShapeDtypeStruct((half - SOON, BLK, BLK), BF),
            jax.ShapeDtypeStruct((BLK, BLK), F32),
        ],
        pltpu.VMEM,
        [
            pltpu.VMEM((num_dst + 1, BLK, BLK), F32),
            pltpu.VMEM(blocks.shape, BF),
            pltpu.SemaphoreType.DMA((slots // CHUNK,)),
        ],
    )


def middle_kernel(parts, weight, cotangent, activated, message):
    dot = lambda a, b: jnp.dot(a, b, preferred_element_type=F32)
    spread = wide(parts[0])
    for k in range(1, parts.shape[0]):
        spread = spread + wide(parts[k])
    high, low = split(spread)
    preact = dot(high, weight[...]) + dot(low, weight[...])
    activated[...] = (preact * jax.nn.sigmoid(preact)).astype(BF)
    delta = wide(cotangent[...]) * silu_grad(preact)
    rounded = delta.astype(BF)
    blocks = [delta[b * BLK : (b + 1) * BLK].T.astype(BF) for b in range(BPD)]
    blocks.append((dot(high.T, rounded) + dot(low.T, rounded)).astype(BF))
    for k in range(message.shape[0]):
        for b, block in enumerate(blocks):
            message[k, b] = block


def middle(parts, weight, cotangent):
    vmem = pl.BlockSpec(memory_space=pltpu.VMEM)
    return pl.pallas_call(
        middle_kernel,
        name="middle",
        in_specs=[vmem] * 3,
        out_specs=[vmem] * 2,
        out_shape=[
            jax.ShapeDtypeStruct(cotangent.shape, BF),
            jax.ShapeDtypeStruct((parts.shape[0], BPD + 1, BLK, BLK), BF),
        ],
        compiler_params=pltpu.CompilerParams(vmem_limit_bytes=VMEM_LIMIT),
        cost_estimate=pl.CostEstimate(
            flops=8 * cotangent.size * BLK, bytes_accessed=4 << 20, transcendentals=cotangent.size
        ),
    )(parts, weight, cotangent)


def gather_rows(own):
    mate = row_swap(own, 2)
    up1, down1 = z_shift(own, 1), z_shift(own, -1)
    mate_up1, mate_down1 = z_shift(own, 1, 2), z_shift(own, -1, 2)
    up2, down2 = z_shift(cat(up1, mate_up1), 1), z_shift(cat(down1, mate_down1), -1)
    up3, down3 = z_shift(up2, 1), z_shift(down2, -1)
    up4 = cat(up3[:HALF], up3[BPD : BPD + HALF])
    down4 = cat(down3[HALF:BPD], down3[BPD + HALF :])
    groups = [
        cat(own, mate, up1, mate_up1),
        cat(down1, mate_down1, up2),
        cat(down2, up3),
        down3,
    ]
    groups, up4, down4 = lax.optimization_barrier((groups, up4, down4))
    up4, down4 = z_shift(up4, 1), z_shift(down4, -1)
    groups.append(cat(up4[:HALF], down4[:HALF], up4[HALF:], down4[HALF:]))
    return groups + [row_swap(group, 1) for group in groups]


def scatter_rows(keep, soon, later, sums):
    soon, later = row_swap(soon, 1), row_swap(later, 1)
    tag = (sums + wide(soon[SOON]) + wide(soon[SOON + 1])).astype(BF)[None]
    seen_up, seen_down = [], []

    def term(d, x, lo=0, hi=BPD):
        at = ORDER.index((d, x)) * BPD
        arrived, first = (soon, at) if at < SOON else (later, at - SOON)
        return wide(keep[at + lo : at + hi]) + wide(arrived[first + lo : first + hi])

    def step(up, down, up_tag, down_tag, ahead=()):
        up = cat(*[part.astype(BF) for part in up], up_tag)
        down = cat(*[part.astype(BF) for part in down], down_tag)
        up, down, ahead = lax.optimization_barrier((up, down, ahead))
        up, down = z_shift(up, 1), z_shift(down, -1)
        up_tag, down_tag = lax.optimization_barrier((up[-1:], down[-1:]))
        seen_up.append(up_tag)
        seen_down.append(down_tag)
        return wide(up[:-1]), wide(down[:-1]), up_tag, down_tag, ahead

    def front(value):
        return jnp.pad(value, ((0, HALF), (0, 0), (0, 0)))

    def back(value):
        return jnp.pad(value, ((HALF, 0), (0, 0), (0, 0)))

    up, down, ut, dt, _ = step([term(4, 1, 0, HALF)], [term(4, 1, HALF)], tag, tag)
    up, down, ut, dt, _ = step(
        [term(3, 1) + front(up), term(4, 0, 0, HALF)],
        [term(4, 0, HALF), term(5, 1) + back(down)],
        ut,
        dt,
    )
    up, down, ut, dt, ahead = step(
        [term(2, 1) + up[:BPD], term(3, 0) + front(up[BPD:])],
        [term(5, 0) + back(down[:HALF]), term(6, 1) + down[HALF:]],
        ut,
        dt,
        [term(1, 1), term(2, 0), term(6, 0), term(7, 1)],
    )
    up, down, ut, dt, ahead = step(
        [ahead[0] + up[:BPD], ahead[1] + up[BPD:]],
        [ahead[2] + down[:BPD], ahead[3] + down[BPD:]],
        ut,
        dt,
        [term(0, 1), term(1, 0), term(7, 0), term(0, 0)],
    )
    near = [tag] + seen_up + seen_down[: NZ // 2 - 1][::-1]
    z = lax.axis_index("row") // 4
    summed = jnp.zeros((BLK, BLK), F32)
    for k in range(NZ):
        d = (z - k) % NZ
        chosen = near[0][0]
        for n in range(1, NZ):
            chosen = jnp.where(d == n, near[n][0], chosen)
        summed = summed + wide(chosen)
    high = lax.optimization_barrier(summed.astype(BF))
    theirs = ahead[0] + up[:BPD] + down[BPD:]
    up = (ahead[1] + up[BPD:]).astype(BF)
    down = (ahead[2] + down[:BPD]).astype(BF)
    up, down = lax.optimization_barrier((up, down))
    up, down = z_shift(up, 1), z_shift(down, -1)
    mate = row_swap(cat(theirs.astype(BF), high[None]), 2)
    near = lax.optimization_barrier(ahead[3] + wide(up) + wide(down))
    return near, mate, high


def finish_kernel(scale, near, mate, high, weight, feature_grad, weight_grad):
    weight_grad[...] = (wide(high[...]) + wide(mate[BPD])) * scale
    for b in range(BPD):
        grad = (near[b] + wide(mate[b])).T.astype(BF)
        out = lax.dot_general(
            grad, weight[...], (((1,), (1,)), ((), ())), preferred_element_type=F32
        )
        feature_grad[b * BLK : (b + 1) * BLK] = out.astype(BF)


def finish(near, mate, high, weight, scale):
    vmem = pl.BlockSpec(memory_space=pltpu.VMEM)
    return pl.pallas_call(
        lambda *refs: finish_kernel(scale, *refs),
        name="finish",
        in_specs=[vmem] * 4,
        out_specs=[vmem] * 2,
        out_shape=[
            jax.ShapeDtypeStruct((BPD * BLK, BLK), BF),
            jax.ShapeDtypeStruct((BLK, BLK), F32),
        ],
        compiler_params=pltpu.CompilerParams(vmem_limit_bytes=VMEM_LIMIT),
        cost_estimate=pl.CostEstimate(
            flops=2 * BPD * BLK**3, bytes_accessed=1 << 20, transcendentals=0
        ),
    )(near, mate, high, weight)


def per_device(features, weight, adj_values, block_coords, block_counts, cotangent):
    blocks = adj_values[0, 0]
    coords = block_coords[0, 0]
    count = block_counts[0]
    slots = blocks.shape[0]
    row_devices = lax.axis_size("row")
    col_devices = lax.axis_size("col")
    row_blocks = col_devices * BPD
    col_blocks = row_devices * BPD
    nodes = features.shape[0]

    me = lax.axis_index("row")
    owner = coords[1] // BPD
    apart = (owner ^ me) & 3
    inner = coords[1] % BPD
    core_part = (apart & 1) * (col_blocks // 2)
    distance = (me // 4 - owner // 4) % NZ * 2 + (apart >> 1)
    from_place = core_part + inner
    for k, place in enumerate(place for pair in PLACES for place in pair):
        from_place = from_place + jnp.where(distance == k, place, 0)
    to_place = core_part + inner
    toward = (owner // 4 - me // 4) % NZ * 2 + (apart >> 1)
    for k, (d, x) in enumerate(ORDER):
        to_place = to_place + jnp.where(toward == 2 * d + x, k * BPD, 0)
    live = jnp.arange(slots, dtype=jnp.int32) < count[0]
    forward_dst = jnp.where(live, coords[0], row_blocks)
    backward_dst = jnp.where(live, to_place, col_blocks)
    delta_at = coords[0] // BPD * (BPD + 1) + coords[0] % BPD

    pieces = gather_rows(features.reshape(BPD, BLK, BLK))
    partial = forward_product(blocks, forward_dst, from_place, count, pieces, row_blocks)
    parts = lax.all_to_all(partial.reshape(col_devices, nodes, BLK), "col", 0, 0)
    activated, message = middle(parts, weight, cotangent)
    every = lax.all_to_all(message, "col", 0, 0).reshape(-1, BLK, BLK)
    sums = backward_product(blocks, backward_dst, delta_at, count, every, col_blocks)
    grad_scale = float(nodes * row_devices * col_devices) ** (-0.5)
    feature_grad, weight_grad = finish(*scatter_rows(*sums), weight, grad_scale)
    return activated, feature_grad, weight_grad


def solution(mesh):
    in_specs = (
        P(("row", "col"), None),
        P(),
        P("row", "col", None, None, None),
        P("row", "col", None, None),
        P("row", "col"),
        P(("row", "col"), None),
    )
    out_specs = (P(("row", "col"), None), P(("row", "col"), None), P())
    return jax.shard_map(
        per_device, mesh=mesh, in_specs=in_specs, out_specs=out_specs, check_vma=False
    )
```

```python
import jax
import jax.numpy as jnp
from jax import lax
from jax.experimental import pallas as pl
from jax.experimental.pallas import tpu as pltpu
from jax.sharding import PartitionSpec as P

NZ = 8
BLK = 128
BPD = 4
HALF = 2
CHUNK = 64
UNROLL = 64
VMEM_LIMIT = 24 << 20
BF = jnp.bfloat16
F32 = jnp.float32

PLACES = ((0, 4), (8, 16), (20, 32), (36, 48), (52, 60), (40, 56), (24, 44), (12, 28))


ORDER = (
    (4, 1), (3, 1), (5, 1), (4, 0), (2, 1), (6, 1), (3, 0), (5, 0),
    (1, 1), (7, 1), (2, 0), (6, 0), (0, 1), (1, 0), (7, 0), (0, 0),
)
SOON = 4 * BPD


def silu_grad(values):
    sigmoid_z = jax.nn.sigmoid(values)
    return sigmoid_z * (1.0 + values * (1.0 - sigmoid_z))


def wide(value):
    return value.astype(F32)


def cat(*values):
    return jnp.concatenate(values, axis=0)


def z_shift(value, step):
    perm = [(r, ((r // 4 + step) % NZ) * 4 + r % 4) for r in range(4 * NZ)]
    return lax.ppermute(value, "row", perm)


def row_swap(value, mask):
    return lax.ppermute(value, "row", [(r, r ^ mask) for r in range(4 * NZ)])


def split(value):
    high = value.astype(BF)
    return high, (value - wide(high)).astype(BF)


def add_products(x_first, dst, src, count, blocks, held, acc, slots, sems):
    per_chunk = CHUNK // UNROLL
    groups = (jnp.clip(count[0], 0, slots.shape[0]) + UNROLL - 1) // UNROLL

    def body(j, carry):
        products = []
        for u in range(UNROLL):
            s = j * UNROLL + u
            a, x = slots[s], held[src[s]]
            pair = (x, a) if x_first else (a, x)
            products.append(jnp.dot(*pair, preferred_element_type=F32))
        for u in range(UNROLL):
            acc[dst[j * UNROLL + u]] += products[u]
        return carry

    def chunk(c, carry):
        load(blocks, slots, sems, c).wait()
        lax.fori_loop(c * per_chunk, jnp.minimum((c + 1) * per_chunk, groups), body, 0)
        return carry

    lax.fori_loop(0, slots.shape[0] // CHUNK, chunk, 0)


def load(blocks, slots, sems, c):
    part = pl.ds(c * CHUNK, CHUNK)
    return pltpu.make_async_copy(blocks.at[part], slots.at[part], sems.at[c])


def forward_kernel(dst, src, count, blocks, *refs):
    pieces, (out, acc, held, slots, sems, piece_sems) = refs[:-6], refs[-6:]
    for c in range(slots.shape[0] // CHUNK):
        load(blocks, slots, sems, c).start()
    copies, at = [], 0
    for k, piece in enumerate(pieces):
        size = piece.shape[0]
        copies.append(
            pltpu.make_async_copy(piece, held.at[pl.ds(at, size)], piece_sems.at[k])
        )
        at += size
    for copy in copies:
        copy.start()
    acc[...] = jnp.zeros_like(acc)
    for copy in copies:
        copy.wait()
    add_products(False, dst, src, count, blocks, held, acc, slots, sems)
    out[...] = acc[: out.shape[0]].astype(out.dtype)


def backward_kernel(dst, src, count, blocks, every, keep, soon, later, sums, acc, slots, sems):
    for c in range(slots.shape[0] // CHUNK):
        load(blocks, slots, sems, c).start()
    acc[...] = jnp.zeros_like(acc)
    span = BPD + 1
    total = wide(every[BPD])
    for k in range(1, every.shape[0] // span):
        total = total + wide(every[k * span + BPD])
    high, low = split(total)
    half = keep.shape[0]
    soon[SOON], soon[SOON + 1] = high, low
    sums[...] = wide(high) + wide(low)
    add_products(True, dst, src, count, blocks, every, acc, slots, sems)
    keep[...] = acc[:half].astype(keep.dtype)
    soon[:SOON] = acc[half : half + SOON].astype(soon.dtype)
    later[...] = acc[half + SOON : 2 * half].astype(later.dtype)


def product(kernel, name, blocks, dst, src, count, sources, out_shape, source_space, scratch):
    vmem = pl.BlockSpec(memory_space=pltpu.VMEM)
    smem = pl.BlockSpec(memory_space=pltpu.SMEM)
    slots = blocks.shape[0]
    return pl.pallas_call(
        kernel,
        name=name,
        in_specs=[smem] * 3
        + [pl.BlockSpec(memory_space=pltpu.HBM)]
        + [pl.BlockSpec(memory_space=source_space)] * len(sources),
        out_specs=[vmem] * len(out_shape),
        out_shape=out_shape,
        scratch_shapes=scratch,
        compiler_params=pltpu.CompilerParams(vmem_limit_bytes=VMEM_LIMIT),
        cost_estimate=pl.CostEstimate(
            flops=2 * slots * BLK**3, bytes_accessed=14 << 20, transcendentals=0
        ),
    )(dst, src, count, pltpu.with_memory_space_constraint(blocks, pltpu.HBM), *sources)


def forward_product(blocks, dst, src, count, pieces, num_dst):
    slots = blocks.shape[0]
    held = sum(piece.shape[0] for piece in pieces)
    (out,) = product(
        forward_kernel,
        "forward_product",
        blocks,
        dst,
        src,
        count,
        pieces,
        [jax.ShapeDtypeStruct((num_dst, BLK, BLK), BF)],
        pl.ANY,
        [
            pltpu.VMEM((num_dst + 1, BLK, BLK), F32),
            pltpu.VMEM((held, BLK, BLK), BF),
            pltpu.VMEM(blocks.shape, BF),
            pltpu.SemaphoreType.DMA((slots // CHUNK,)),
            pltpu.SemaphoreType.DMA((len(pieces),)),
        ],
    )
    return out


def backward_product(blocks, dst, src, count, every, num_dst):
    slots = blocks.shape[0]
    half = num_dst // 2
    return product(
        backward_kernel,
        "backward_product",
        blocks,
        dst,
        src,
        count,
        [every],
        [
            jax.ShapeDtypeStruct((half, BLK, BLK), BF),
            jax.ShapeDtypeStruct((SOON + 2, BLK, BLK), BF),
            jax.ShapeDtypeStruct((half - SOON, BLK, BLK), BF),
            jax.ShapeDtypeStruct((BLK, BLK), F32),
        ],
        pltpu.VMEM,
        [
            pltpu.VMEM((num_dst + 1, BLK, BLK), F32),
            pltpu.VMEM(blocks.shape, BF),
            pltpu.SemaphoreType.DMA((slots // CHUNK,)),
        ],
    )


def middle_kernel(parts, weight, cotangent, activated, message):
    dot = lambda a, b: jnp.dot(a, b, preferred_element_type=F32)
    spread = wide(parts[0])
    for k in range(1, parts.shape[0]):
        spread = spread + wide(parts[k])
    high, low = split(spread)
    preact = dot(high, weight[...]) + dot(low, weight[...])
    activated[...] = (preact * jax.nn.sigmoid(preact)).astype(BF)
    delta = wide(cotangent[...]) * silu_grad(preact)
    rounded = delta.astype(BF)
    blocks = [delta[b * BLK : (b + 1) * BLK].T.astype(BF) for b in range(BPD)]
    blocks.append((dot(high.T, rounded) + dot(low.T, rounded)).astype(BF))
    for k in range(message.shape[0]):
        for b, block in enumerate(blocks):
            message[k, b] = block


def middle(parts, weight, cotangent):
    vmem = pl.BlockSpec(memory_space=pltpu.VMEM)
    return pl.pallas_call(
        middle_kernel,
        name="middle",
        in_specs=[vmem] * 3,
        out_specs=[vmem] * 2,
        out_shape=[
            jax.ShapeDtypeStruct(cotangent.shape, BF),
            jax.ShapeDtypeStruct((parts.shape[0], BPD + 1, BLK, BLK), BF),
        ],
        compiler_params=pltpu.CompilerParams(vmem_limit_bytes=VMEM_LIMIT),
        cost_estimate=pl.CostEstimate(
            flops=8 * cotangent.size * BLK, bytes_accessed=4 << 20, transcendentals=cotangent.size
        ),
    )(parts, weight, cotangent)


def gather_rows(own):
    mate = row_swap(own, 2)
    up1, down1 = z_shift(own, 1), z_shift(own, -1)
    up2, down2 = z_shift(cat(mate, up1), 1), z_shift(cat(down1, mate), -1)
    up3, down3 = z_shift(up2, 1), z_shift(down2, -1)
    up4, down4 = z_shift(up3[: BPD + HALF], 1), z_shift(down3[HALF:], -1)
    up5, down5 = z_shift(up4[:HALF], 1), z_shift(down4[BPD:], -1)
    groups = [cat(own, mate, up1, down1), cat(up2, down2), cat(up3, down3)]
    groups, up4, down4 = lax.optimization_barrier((groups, up4, down4))
    groups += [cat(up4, down4), cat(up5, down5)]
    return groups + [row_swap(group, 1) for group in groups]


def scatter_rows(keep, soon, later, sums):
    soon, later = row_swap(soon, 1), row_swap(later, 1)
    tag = (sums + wide(soon[SOON]) + wide(soon[SOON + 1])).astype(BF)[None]
    seen_up, seen_down = [], []

    def term(d, x, lo=0, hi=BPD):
        at = ORDER.index((d, x)) * BPD
        arrived, first = (soon, at) if at < SOON else (later, at - SOON)
        return wide(keep[at + lo : at + hi]) + wide(arrived[first + lo : first + hi])

    def step(up, down, up_tag, down_tag, ahead=()):
        up = cat(*[part.astype(BF) for part in up], up_tag)
        down = cat(*[part.astype(BF) for part in down], down_tag)
        up, down, ahead = lax.optimization_barrier((up, down, ahead))
        up, down = z_shift(up, 1), z_shift(down, -1)
        up_tag, down_tag = lax.optimization_barrier((up[-1:], down[-1:]))
        seen_up.append(up_tag)
        seen_down.append(down_tag)
        return wide(up[:-1]), wide(down[:-1]), up_tag, down_tag, ahead

    def front(value):
        return jnp.pad(value, ((0, HALF), (0, 0), (0, 0)))

    def back(value):
        return jnp.pad(value, ((HALF, 0), (0, 0), (0, 0)))

    up, down, ut, dt, _ = step([term(4, 1, 0, HALF)], [term(4, 1, HALF)], tag, tag)
    up, down, ut, dt, _ = step(
        [term(3, 1) + front(up), term(4, 0, 0, HALF)],
        [term(4, 0, HALF), term(5, 1) + back(down)],
        ut,
        dt,
    )
    up, down, ut, dt, ahead = step(
        [term(2, 1) + up[:BPD], term(3, 0) + front(up[BPD:])],
        [term(5, 0) + back(down[:HALF]), term(6, 1) + down[HALF:]],
        ut,
        dt,
        [term(1, 1), term(2, 0), term(6, 0), term(7, 1)],
    )
    up, down, ut, dt, ahead = step(
        [ahead[0] + up[:BPD], ahead[1] + up[BPD:]],
        [ahead[2] + down[:BPD], ahead[3] + down[BPD:]],
        ut,
        dt,
        [term(0, 1), term(1, 0), term(7, 0), term(0, 0)],
    )
    near = [tag] + seen_up + seen_down[: NZ // 2 - 1][::-1]
    z = lax.axis_index("row") // 4
    summed = jnp.zeros((BLK, BLK), F32)
    for k in range(NZ):
        d = (z - k) % NZ
        chosen = near[0][0]
        for n in range(1, NZ):
            chosen = jnp.where(d == n, near[n][0], chosen)
        summed = summed + wide(chosen)
    high = lax.optimization_barrier(summed.astype(BF))
    theirs = ahead[0] + up[:BPD] + down[BPD:]
    up = (ahead[1] + up[BPD:]).astype(BF)
    down = (ahead[2] + down[:BPD]).astype(BF)
    up, down = lax.optimization_barrier((up, down))
    up, down = z_shift(up, 1), z_shift(down, -1)
    mate = row_swap(cat(theirs.astype(BF), high[None]), 2)
    near = lax.optimization_barrier(ahead[3] + wide(up) + wide(down))
    return near, mate, high


def finish_kernel(scale, near, mate, high, weight, feature_grad, weight_grad):
    weight_grad[...] = (wide(high[...]) + wide(mate[BPD])) * scale
    for b in range(BPD):
        grad = (near[b] + wide(mate[b])).T.astype(BF)
        out = lax.dot_general(
            grad, weight[...], (((1,), (1,)), ((), ())), preferred_element_type=F32
        )
        feature_grad[b * BLK : (b + 1) * BLK] = out.astype(BF)


def finish(near, mate, high, weight, scale):
    vmem = pl.BlockSpec(memory_space=pltpu.VMEM)
    return pl.pallas_call(
        lambda *refs: finish_kernel(scale, *refs),
        name="finish",
        in_specs=[vmem] * 4,
        out_specs=[vmem] * 2,
        out_shape=[
            jax.ShapeDtypeStruct((BPD * BLK, BLK), BF),
            jax.ShapeDtypeStruct((BLK, BLK), F32),
        ],
        compiler_params=pltpu.CompilerParams(vmem_limit_bytes=VMEM_LIMIT),
        cost_estimate=pl.CostEstimate(
            flops=2 * BPD * BLK**3, bytes_accessed=1 << 20, transcendentals=0
        ),
    )(near, mate, high, weight)


def per_device(features, weight, adj_values, block_coords, block_counts, cotangent):
    blocks = adj_values[0, 0]
    coords = block_coords[0, 0]
    count = block_counts[0]
    slots = blocks.shape[0]
    row_devices = lax.axis_size("row")
    col_devices = lax.axis_size("col")
    row_blocks = col_devices * BPD
    col_blocks = row_devices * BPD
    nodes = features.shape[0]

    me = lax.axis_index("row")
    owner = coords[1] // BPD
    apart = (owner ^ me) & 3
    inner = coords[1] % BPD
    core_part = (apart & 1) * (col_blocks // 2)
    distance = (me // 4 - owner // 4) % NZ * 2 + (apart >> 1)
    from_place = core_part + inner
    for k, place in enumerate(place for pair in PLACES for place in pair):
        from_place = from_place + jnp.where(distance == k, place, 0)
    to_place = core_part + inner
    toward = (owner // 4 - me // 4) % NZ * 2 + (apart >> 1)
    for k, (d, x) in enumerate(ORDER):
        to_place = to_place + jnp.where(toward == 2 * d + x, k * BPD, 0)
    live = jnp.arange(slots, dtype=jnp.int32) < count[0]
    forward_dst = jnp.where(live, coords[0], row_blocks)
    backward_dst = jnp.where(live, to_place, col_blocks)
    delta_at = coords[0] // BPD * (BPD + 1) + coords[0] % BPD

    pieces = gather_rows(features.reshape(BPD, BLK, BLK))
    partial = forward_product(blocks, forward_dst, from_place, count, pieces, row_blocks)
    parts = lax.all_to_all(partial.reshape(col_devices, nodes, BLK), "col", 0, 0)
    activated, message = middle(parts, weight, cotangent)
    every = lax.all_to_all(message, "col", 0, 0).reshape(-1, BLK, BLK)
    sums = backward_product(blocks, backward_dst, delta_at, count, every, col_blocks)
    grad_scale = float(nodes * row_devices * col_devices) ** (-0.5)
    feature_grad, weight_grad = finish(*scatter_rows(*sums), weight, grad_scale)
    return activated, feature_grad, weight_grad


def solution(mesh):
    in_specs = (
        P(("row", "col"), None),
        P(),
        P("row", "col", None, None, None),
        P("row", "col", None, None),
        P("row", "col"),
        P(("row", "col"), None),
    )
    out_specs = (P(("row", "col"), None), P(("row", "col"), None), P())
    return jax.shard_map(
        per_device, mesh=mesh, in_specs=in_specs, out_specs=out_specs, check_vma=False
    )
```
